256 devices in a mesh: row: 8 (over x, core), col: 32 (over y, z).
Axes of the slice: x: 4, y: 4, z: 8, core: 2. Of those that a mesh axis runs over, the one named last changes fastest.
Arguments:
- blocks: float32 [2048, 8, 128, 128], P(('row', 'col')), may hold values from -2 to 2
- prolong: float32 [2048, 128, 128], P(('row', 'col')), may hold values from -0.5 to 0.5
- counts: int32 [2048], P(('row', 'col')), may hold values from 1 to 8
- columns: int32 [2048, 8], P(('row', 'col')), may hold values from 0 to 255, as said below
- aggregates: int32 [2048], P(('row', 'col')), may hold values from 0 to 1
Outputs:
- coarse_operator: float32 [512, 64, 128, 128], P(('row', 'col'))
The draws below stay inside these ranges and needn't reach their ends.
Inputs may be any that keep to these rules, and one draw needn't show every extreme that they name: Over all slots of the 8 rows of one device, the columns that fall among the rows of any one device of the slab (columns // 8 equal) take at most 2 distinct values; every device reaches 2 for some such device.
All inputs are finite; a program needn't handle non-finite values.
Results may differ from the reference program's by a relative error of at most 0.0003.
Values sent between devices are 32-bit elements; how exact they have to be, the bound alone decides.
No kernel may reach another device: no remote copies, remote signals or barrier semaphores. Data moves between devices by JAX's collectives and lax.ppermute only.
A program may use at most 64 MiB of HBM per device.

```python
import jax
import jax.numpy as jnp
from jax import lax

TB = 128
K = 8
BR = 8
AGD = 2
CAP = 2
NB = 2048
N_COL = 32


def draw_columns(key, part):
    key_owner = jax.random.fold_in(key, 11)
    key_base = jax.random.fold_in(key, 12)
    key_offset = jax.random.fold_in(key, 13)
    owner = jax.random.randint(key_owner, (NB, K), 0, N_COL, dtype=jnp.int32)
    offset = jax.random.randint(key_offset, (NB, K), 0, CAP, dtype=jnp.int32)
    base = jax.random.randint(key_base, (NB // BR, N_COL), 0, BR, dtype=jnp.int32)
    base_rows = jnp.repeat(base, BR, axis=0)
    first_row = jnp.arange(NB, dtype=jnp.int32) % BR == 0
    first_slots = jnp.arange(K, dtype=jnp.int32) < CAP
    forced = first_row[:, None] & first_slots[None, :]
    owner = jnp.where(forced, owner[:, :1], owner)
    offset = jnp.where(forced, jnp.arange(K, dtype=jnp.int32)[None, :], offset)
    chosen = jnp.take_along_axis(base_rows, owner, axis=1)
    local = (chosen + offset) % BR
    return (owner * BR + local).astype(jnp.int32)


def place_ends(entries, stream_key, smallest, largest):
    longest = entries.shape.index(max(entries.shape))
    spots = []
    for shift in (0, 1):
        where = [jax.random.randint(jax.random.fold_in(stream_key, axis), (), 0, length) for axis, length in enumerate(entries.shape)]
        where[longest] = (where[longest] + shift) % entries.shape[longest]
        spots.append(tuple(where))
    return entries.at[spots[0]].set(smallest).at[spots[1]].set(largest)


def block_scale(key, dims, shards, low, top_value):
    level, own = 1.0, jax.random.fold_in(key, 6)
    for axis_at, blocks in shards:
        steps = jnp.exp(jax.random.uniform(jax.random.fold_in(own, axis_at), (blocks,), jnp.float32, low / len(shards), top_value / len(shards)))
        level = level * jnp.repeat(steps, dims[axis_at] // blocks).reshape([-1 if axis == axis_at else 1 for axis in range(len(dims))])
    return level


def bell_draw(rng, extent, width, most, pieces=(), kind=jnp.bfloat16):
    drawn = jax.random.normal(rng, extent, jnp.float32) * width
    if len(pieces) > 0:
        drawn = block_scale(rng, extent, pieces, -0.22, 0.18) * drawn
    return jnp.clip(drawn, min=-most, max=most).astype(kind)


def setup_inputs(seed: int = 0) -> dict:
    arg_keys = jax.random.split(jax.random.key(seed), 6)
    blocks = bell_draw(arg_keys[0], (NB, K, TB, TB), 0.25, 2.0, ((0, 256),), jnp.float32)
    prolong = bell_draw(arg_keys[1], (NB, TB, TB), TB ** -0.5, 0.5, ((0, 256),), jnp.float32)
    counts = place_ends(jax.random.randint(arg_keys[2], (NB,), 1, K + 1), jax.random.fold_in(arg_keys[2], 1), 1, K).astype(jnp.int32)
    columns = draw_columns(jax.random.fold_in(arg_keys[5], 71), 0)
    aggregates = place_ends(jax.random.randint(arg_keys[4], (NB,), 0, AGD), jax.random.fold_in(arg_keys[4], 1), 0, AGD - 1).astype(jnp.int32)
    return {"blocks": blocks, "prolong": prolong, "counts": counts, "columns": columns, "aggregates": aggregates}


def reference(blocks, prolong, counts, columns, aggregates):
    fine = BR * N_COL
    wide = AGD * N_COL
    slots = blocks.shape[1]
    tile = blocks.shape[-1]
    groups = blocks.shape[0] // BR
    high = lax.Precision.HIGHEST

    def one_group(group):
        start = (group * BR).astype(jnp.int32)
        tiles = lax.dynamic_slice_in_dim(blocks, start, BR, 0)
        own = lax.dynamic_slice_in_dim(prolong, start, BR, 0)
        live_count = lax.dynamic_slice_in_dim(counts, start, BR, 0)
        cols = lax.dynamic_slice_in_dim(columns, start, BR, 0)
        own_agg = lax.dynamic_slice_in_dim(aggregates, start, BR, 0)
        base = ((group // N_COL) * fine).astype(jnp.int32)
        joined = (base + cols).astype(jnp.int32)
        picked = jnp.take(prolong, joined, axis=0)
        col_agg = jnp.take(aggregates, joined, axis=0)
        coarse_col = (cols // BR) * AGD + col_agg
        inner = jnp.einsum('bkxy,bkyz->bkxz', tiles, picked, precision=high)
        terms = jnp.einsum('bxw,bkxz->bkwz', own, inner, precision=high)
        live = (jnp.arange(slots, dtype=jnp.int32)[None, :] < live_count[:, None]).astype(blocks.dtype)
        col_hot = (coarse_col[:, :, None] == jnp.arange(wide, dtype=jnp.int32)[None, None, :]).astype(blocks.dtype) * live[:, :, None]
        row_hot = (own_agg[:, None] == jnp.arange(AGD, dtype=jnp.int32)[None, :]).astype(blocks.dtype)
        weights = (row_hot[:, None, :, None] * col_hot[:, :, None, :]).reshape(BR * slots, AGD * wide)
        flat_terms = terms.reshape(BR * slots, tile * tile)
        summed = jnp.dot(weights.T, flat_terms, precision=high)
        return summed.reshape(AGD, wide, tile, tile)

    galerkin = lax.map(one_group, jnp.arange(groups, dtype=jnp.int32))
    galerkin = galerkin.reshape(groups * AGD, wide, tile, tile)
    sums = jnp.sum(jnp.abs(galerkin), axis=(1, 3))
    bound = jnp.max(sums)
    return galerkin / (bound + 1e-6)
```

```python
import functools

import jax
import jax.numpy as jnp
from jax import lax
from jax.experimental import pallas as pl
from jax.experimental.pallas import tpu as pltpu
from jax.sharding import Mesh
from jax.sharding import PartitionSpec as P

AGD = 2
CAP = 2
COL = ("col_0", "col_1")
ROW_COL = ("row_0", "row_1", "col_0", "col_1")
ANY = pl.BlockSpec(memory_space=pl.ANY)
SMEM = pl.BlockSpec(memory_space=pltpu.SMEM)
VMEM = pl.BlockSpec(memory_space=pltpu.VMEM)
MIB = 1 << 20


def split(x):
    hi = x.astype(jnp.bfloat16)
    lo = (x - hi.astype(jnp.float32)).astype(jnp.bfloat16)
    return hi, lo


def dot3(a, b):
    d = functools.partial(jnp.dot, preferred_element_type=jnp.float32)
    return d(a[0], b[0]) + (d(a[0], b[1]) + d(a[1], b[0]))


def inner_kernel(blocks_ref, prolong_ref, out_ref):
    left = split(prolong_ref[0].T)
    for k in range(blocks_ref.shape[1]):
        out_ref[0, k] = dot3(left, split(blocks_ref[0, k]))


def inner_products(blocks, prolong):
    rows, slots, tile, _ = blocks.shape
    return pl.pallas_call(
        inner_kernel,
        grid=(rows,),
        in_specs=[
            pl.BlockSpec((1, slots, tile, tile), lambda i: (i, 0, 0, 0)),
            pl.BlockSpec((1, tile, tile), lambda i: (i, 0, 0)),
        ],
        out_specs=pl.BlockSpec((1, slots, tile, tile), lambda i: (i, 0, 0, 0)),
        out_shape=jax.ShapeDtypeStruct(blocks.shape, jnp.float32),
        cost_estimate=pl.CostEstimate(
            flops=6 * rows * slots * tile**3, bytes_accessed=9 * MIB, transcendentals=0
        ),
        name="inner",
    )(blocks, prolong)


def pick_kernel(steps, halves, pick_ref, a_ref, b_ref, out_ref, sems):
    peers = out_ref.shape[0]

    def copy(src, tile, y, s, p):
        at = (y * out_ref.shape[1] + s) * CAP + p
        return pltpu.make_async_copy(src.at[tile], out_ref.at[y, s, p], sems.at[at])

    places = [(y, s, p) for y in range(peers) for s in range(len(steps)) for p in range(CAP)]
    for y, s, p in places:
        tile = pick_ref[y, 2 * steps[s] + p]
        if halves:
            half = a_ref.shape[0]

            @pl.when(tile < half)
            def _():
                copy(a_ref, tile, y, s, p).start()

            @pl.when(tile >= half)
            def _():
                copy(b_ref, tile - half, y, s, p).start()
        else:
            copy((a_ref, b_ref)[s], tile, y, s, p).start()
    for y, s, p in places:
        copy(a_ref, 0, y, s, p).wait()


def pick(picks, a, b, steps, halves=False):
    peers = picks.shape[0]
    shape = (peers, len(steps), CAP, *a.shape[1:])
    return pl.pallas_call(
        functools.partial(pick_kernel, steps, halves),
        in_specs=[SMEM, ANY, ANY],
        out_specs=ANY,
        out_shape=jax.ShapeDtypeStruct(shape, jnp.float32),
        scratch_shapes=[pltpu.SemaphoreType.DMA((peers * len(steps) * CAP,))],
        name="pick",
    )(picks, a, b)


def terms_kernel(slot_ref, inner_ref, *refs):
    parts, (out_ref, most_ref, tiles, sems) = refs[:-4], refs[-4:]
    at = 0
    copies = []
    for n, part in enumerate(parts):
        count = part.shape[0]
        copies.append(pltpu.make_async_copy(part, tiles.at[pl.ds(at, count)], sems.at[n]))
        at += count
    for c in copies:
        c.start()
    wide = out_ref.shape[0]
    tile = out_ref.shape[-1]

    def clear(e, _):
        out_ref[e] = jnp.zeros((tile, tile), jnp.float32)
        return 0

    lax.fori_loop(0, wide, clear, 0)
    for c in copies:
        c.wait()

    def one(s, _):
        @pl.when(slot_ref[0, s] >= 0)
        def _():
            term = dot3(split(inner_ref[s]), split(tiles[slot_ref[0, s]]))
            e = slot_ref[1, s]
            out_ref[e] = out_ref[e] + term

        return 0

    lax.fori_loop(0, inner_ref.shape[0], one, 0)
    half = wide // AGD
    most = jnp.float32(0)
    for c in range(AGD):
        total = lax.fori_loop(
            0, half, lambda e, t: t + jnp.abs(out_ref[c * half + e]), jnp.zeros((tile, tile), jnp.float32)
        )
        most = jnp.maximum(most, jnp.max(jnp.sum(total, axis=1)))
    most_ref[...] = jnp.full(most_ref.shape, most, jnp.float32)


def sum_terms(slots, inner, parts, wide):
    tile = inner.shape[-1]
    return pl.pallas_call(
        terms_kernel,
        in_specs=[SMEM, VMEM] + [ANY] * len(parts),
        out_specs=[VMEM, VMEM],
        out_shape=[
            jax.ShapeDtypeStruct((wide, tile, tile), jnp.float32),
            jax.ShapeDtypeStruct((1, tile), jnp.float32),
        ],
        scratch_shapes=[
            pltpu.VMEM((sum(p.shape[0] for p in parts), tile, tile), jnp.float32),
            pltpu.SemaphoreType.DMA((len(parts),)),
        ],
        compiler_params=pltpu.CompilerParams(vmem_limit_bytes=40 * MIB),
        name="terms",
    )(slots, inner, *parts)


def wanted_ends(cols, live, owners, rows):
    hit = live[:, :, None] & (cols[:, :, None] // rows == owners[None, None, :])
    local = (cols % rows)[:, :, None]
    low = jnp.min(jnp.where(hit, local, rows - 1), axis=1)
    high = jnp.max(jnp.where(hit, local, 0), axis=1)
    return low, high


def per_device(blocks, prolong, counts, columns, aggregates):
    rows, slots = columns.shape
    tile = blocks.shape[-1]
    ny, nz = lax.axis_size("col_0"), lax.axis_size("col_1")
    my_y, my_z = lax.axis_index("col_0"), lax.axis_index("col_1")
    peers = ny * nz
    flat = rows * slots
    live = jnp.arange(slots, dtype=jnp.int32)[None, :] < counts[:, None]
    live = live.reshape(1, flat)
    cols = columns.reshape(1, flat)
    note = jnp.concatenate([jnp.where(live, cols, -1), aggregates[None, :]], axis=1)
    note = jnp.pad(note, ((0, 0), (0, 128 - flat - rows)))
    notes = lax.all_to_all(
        jnp.broadcast_to(note, (peers, 128)), COL, split_axis=0, concat_axis=0, tiled=True
    )
    inner = inner_products(blocks, prolong)
    around = [[(i, (i + d) % nz) for i in range(nz)] for d in (1, -1)]
    hop = lambda x, way: lax.ppermute(x, "col_1", around[way])
    theirs = lax.dynamic_slice_in_dim(notes.reshape(ny, nz, 128), my_z, 1, 1)[:, 0, :flat]
    apart = jnp.arange(nz, dtype=jnp.int32)
    owners = my_y * nz + (my_z + apart) % nz
    low, high = wanted_ends(theirs, theirs >= 0, owners, rows)
    picks = jnp.stack([low, high], axis=-1).reshape(ny, nz * CAP)
    swap = lambda x: lax.all_to_all(x, "col_0", split_axis=0, concat_axis=0, tiled=True)
    parts = [swap(pick(picks, prolong, prolong, (0,)))]
    up = down = prolong
    for r in range(1, nz // 2):
        up, down = hop(up, 0), hop(down, 1)
        parts.append(swap(pick(picks, up, down, (nz - r, r))))
    up, down = hop(up[: rows // 2], 0), hop(down[rows // 2 :], 1)
    parts.append(swap(pick(picks, up, down, (nz // 2,), halves=True)))
    parts = [p.reshape(-1, tile, tile) for p in parts]
    owner, within = cols // rows, cols % rows
    same = (owner.T == owner) & live
    first = jnp.min(jnp.where(same, within, rows), axis=1)[None, :]
    second = (within > first).astype(jnp.int32)
    ahead = (owner % nz - my_z) % nz
    r = jnp.minimum(ahead, nz - ahead)
    alone = (r == 0) | (r == nz // 2)
    base = jnp.where(r == 0, 0, (2 * r - 1) * ny * CAP)
    at_set = jnp.where(alone, owner // nz, owner // nz * 2 + (ahead == r).astype(jnp.int32))
    source = jnp.where(live, base + at_set * CAP + second, -1)
    slab_agg = notes[:, flat : flat + rows]
    hot = (owner.T[:, :, None] == jnp.arange(peers)[None, :, None]) & (
        within.T[:, :, None] == jnp.arange(rows)[None, None, :]
    )
    col_agg = jnp.sum(jnp.where(hot, slab_agg[None], 0), axis=(1, 2))[None, :]
    row_agg = jnp.broadcast_to(aggregates[:, None], (rows, slots)).reshape(1, flat)
    target = row_agg * (AGD * peers) + owner * AGD + col_agg
    where = jnp.concatenate([source, target], axis=0).astype(jnp.int32)
    galerkin, most = sum_terms(where, inner.reshape(flat, tile, tile), parts, AGD * AGD * peers)
    everyone = lax.axis_size(ROW_COL)
    all_most = lax.all_to_all(
        jnp.broadcast_to(most, (everyone, tile)), ROW_COL, split_axis=0, concat_axis=0, tiled=True
    )
    bound = jnp.max(all_most)
    return galerkin.reshape(AGD, AGD * peers, tile, tile) / (bound + 1e-06)


def solution(mesh):
    torus = Mesh(mesh.devices.reshape(4, 2, 4, 8), ("row_0", "row_1", "col_0", "col_1"))
    placed = (
        P(ROW_COL, None, None, None),
        P(ROW_COL, None, None),
        P(ROW_COL),
        P(ROW_COL, None),
        P(ROW_COL),
    )
    return jax.shard_map(
        per_device,
        mesh=torus,
        in_specs=placed,
        out_specs=P(ROW_COL, None, None, None),
        check_vma=False,
    )
```

```python
import functools

import jax
import jax.numpy as jnp
from jax import lax
from jax.experimental import pallas as pl
from jax.experimental.pallas import tpu as pltpu
from jax.sharding import Mesh
from jax.sharding import PartitionSpec as P

AGD = 2
CAP = 2
COL = ("col_0", "col_1")
ROW_COL = ("row_0", "row_1", "col_0", "col_1")
ANY = pl.BlockSpec(memory_space=pl.ANY)
SMEM = pl.BlockSpec(memory_space=pltpu.SMEM)
VMEM = pl.BlockSpec(memory_space=pltpu.VMEM)
HBM = pl.BlockSpec(memory_space=pltpu.HBM)
MIB = 1 << 20
UNROLL = 4
CUTS = (1,2)
MERGED = 1
EARLY = 0
LIMIT = 60


def split(x, axis):
    hi = x.astype(jnp.bfloat16)
    lo = (x - hi.astype(jnp.float32)).astype(jnp.bfloat16)
    return jnp.concatenate([hi, lo], axis=axis)


def dot_split(left, right):
    n = right.shape[0]
    four = jnp.dot(left, right, preferred_element_type=jnp.float32)
    return four[:n, :n] + ((four[:n, n:] + four[n:, :n]) + four[n:, n:])


def params(mib):
    return pltpu.CompilerParams(vmem_limit_bytes=mib * MIB)


def inner_kernel(blocks_ref, prolong_ref, out_ref, done_ref):
    left = split(prolong_ref[0].T, 0)
    for k in range(blocks_ref.shape[1]):
        out_ref[0, k] = split(dot_split(left, split(blocks_ref[0, k], 1)), 0)
    done_ref[...] = jnp.zeros_like(done_ref)


def inner_products(blocks, prolong):
    rows, slots, tile, _ = blocks.shape
    return pl.pallas_call(
        inner_kernel,
        grid=(rows,),
        in_specs=[
            pl.BlockSpec((1, slots, tile, tile), lambda i: (i, 0, 0, 0)),
            pl.BlockSpec((1, tile, tile), lambda i: (i, 0, 0)),
        ],
        out_specs=[
            pl.BlockSpec((1, slots, 2 * tile, tile), lambda i: (i, 0, 0, 0)),
            pl.BlockSpec((8, tile), lambda i: (0, 0)),
        ],
        out_shape=[
            pltpu.HBM((rows, slots, 2 * tile, tile), jnp.bfloat16),
            jax.ShapeDtypeStruct((8, tile), jnp.float32),
        ],
        cost_estimate=pl.CostEstimate(
            flops=8 * rows * slots * tile**3, bytes_accessed=9 * MIB, transcendentals=0
        ),
        compiler_params=params(LIMIT),
        name="inner",
    )(blocks, prolong)


def pick_kernel(steps, apart, pick_ref, at_ref, *refs):
    peers = pick_ref.shape[0]
    count = peers if apart else 1
    sources, outs, (sets, sems) = refs[: len(steps)], refs[-2 - count : -2], refs[-2:]
    loads, place = [], {}
    at = 0
    for n, step in enumerate(steps):
        place[step] = place.get(step, at)
        count = sources[n].shape[0]
        loads.append(
            pltpu.make_async_copy(sources[n], sets.at[pl.ds(at, count)], sems.at[n])
        )
        at += count
    for load in loads:
        load.start()
    for n, load in enumerate(loads):
        load.wait()
        if steps[n] in steps[n + 1 :]:
            continue
        s = list(place).index(steps[n])
        for y in range(peers):
            for p in range(CAP):
                if apart:
                    out, peer = outs[y], (at_ref[0] + y) % peers
                else:
                    out, peer = outs[0].at[y], y
                out[CAP * s + p] = sets[place[steps[n]] + pick_ref[peer, CAP * steps[n] + p]]


def pick(picks, at, sets, steps, apart, after):
    peers = picks.shape[0]
    shape = (len(set(steps)) * CAP, *sets[0].shape[1:])
    shapes = [pltpu.HBM(shape, jnp.float32)] * peers
    return pl.pallas_call(
        functools.partial(pick_kernel, steps, apart),
        in_specs=[SMEM, SMEM] + [ANY] * (len(sets) + len(after)),
        out_specs=[VMEM] * peers if apart else [VMEM],
        out_shape=shapes if apart else [pltpu.HBM((peers, *shape), jnp.float32)],
        scratch_shapes=[
            pltpu.VMEM((sum(x.shape[0] for x in sets), *shape[1:]), jnp.float32),
            pltpu.SemaphoreType.DMA((len(sets),)),
        ],
        cost_estimate=pl.CostEstimate(flops=0, bytes_accessed=8 * MIB, transcendentals=0),
        compiler_params=params(LIMIT),
        name="pick",
    )(picks, at, *sets, *after)


def terms_kernel(slot_ref, inner_ref, *refs):
    parts, rest = refs[:-13], refs[-13:]
    out_ref, used_ref, most_ref, left, held, right, sums, most, ids, agg_ref, sem, sems, part_sems = rest
    wide = out_ref.shape[0]
    tile = out_ref.shape[-1]
    load = pltpu.make_async_copy(inner_ref, left, sem)
    copies = []
    at = 0
    for n, part in enumerate(parts):
        count = part.shape[0]
        copies.append(pltpu.make_async_copy(part, held.at[pl.ds(at, count)], part_sems.at[n]))
        copies[-1].start()
        at += count
    load.start()

    def clear(e, _):
        for n in range(8):
            used_ref[8 * e + n] = 0
        return 0

    lax.fori_loop(0, used_ref.shape[0] // 8, clear, 0)
    at = 0
    for part, copy in zip(parts, copies):
        copy.wait()
        for n in range(at, at + part.shape[0]):
            right[n] = split(held[n, :tile], 1)
            ids[n : n + 1] = held[n, tile : tile + 1].astype(jnp.int32)
        at += part.shape[0]
    load.wait()
    look_up = pltpu.make_async_copy(ids, agg_ref, sem)
    look_up.start()
    look_up.wait()
    live = slot_ref[3, 0]

    def some(n, _):
        terms = []
        for m in range(UNROLL):
            s = UNROLL * n + m
            terms.append(dot_split(left[slot_ref[0, s]], right[slot_ref[1, s]]))
        for m in range(UNROLL):
            s = UNROLL * n + m
            e = jnp.where(s < live, slot_ref[2, s] + agg_ref[slot_ref[1, s], 0], wide)

            @pl.when(e < wide)
            def _():
                @pl.when(used_ref[e] == 0)
                def _():
                    count = used_ref[2 * wide]
                    used_ref[e] = 1
                    used_ref[wide + count] = e
                    used_ref[2 * wide] = count + 1
                    sums[e] = jnp.zeros((tile, tile), jnp.float32)

            sums[e] = sums[e] + terms[m]
        return 0

    sums[wide] = jnp.zeros((tile, tile), jnp.float32)
    lax.fori_loop(0, (live + UNROLL - 1) // UNROLL, some, 0)
    most[...] = jnp.zeros_like(most)
    half = wide // AGD
    copy = lambda e: pltpu.make_async_copy(sums.at[e], out_ref.at[e], sems.at[e])

    def look(e):
        copy(e).start()
        most[e // half] = most[e // half] + jnp.abs(sums[e])

    each_used(used_ref, look)
    row_sums = jnp.sum(most[...], axis=2)
    most_ref[...] = jnp.full(most_ref.shape, jnp.max(row_sums), jnp.float32)
    each_used(used_ref, lambda e: copy(e).wait())


def each_used(used_ref, do):
    wide = used_ref.shape[0] // 2 - 4

    def step(n, _):
        do(used_ref[wide + n])
        return 0

    lax.fori_loop(0, used_ref[2 * wide], step, 0)


def sum_terms(slots, inner, parts, wide):
    flat, _, tile = inner.shape
    return pl.pallas_call(
        terms_kernel,
        in_specs=[SMEM, ANY] + [ANY] * len(parts),
        out_specs=[ANY, SMEM, VMEM],
        out_shape=[
            pltpu.HBM((wide, tile, tile), jnp.float32),
            jax.ShapeDtypeStruct((2 * wide + 8,), jnp.int32),
            jax.ShapeDtypeStruct((1, tile), jnp.float32),
        ],
        scratch_shapes=[
            pltpu.VMEM(inner.shape, jnp.bfloat16),
            pltpu.VMEM((flat, *parts[0].shape[1:]), jnp.float32),
            pltpu.VMEM((flat, tile, 2 * tile), jnp.bfloat16),
            pltpu.VMEM((wide + 1, tile, tile), jnp.float32),
            pltpu.VMEM((AGD, tile, tile), jnp.float32),
            pltpu.VMEM((flat, tile), jnp.int32),
            pltpu.SMEM((flat, tile), jnp.int32),
            pltpu.SemaphoreType.DMA,
            pltpu.SemaphoreType.DMA((wide,)),
            pltpu.SemaphoreType.DMA((len(parts),)),
        ],
        cost_estimate=pl.CostEstimate(
            flops=8 * flat * tile**3, bytes_accessed=16 * MIB, transcendentals=0
        ),
        compiler_params=params(LIMIT),
        name="terms",
    )(slots, inner, *parts)


def clear_kernel(used_ref, _, out_ref, zero, sems):
    zero[...] = jnp.zeros_like(zero)
    copy = lambda e: pltpu.make_async_copy(zero, out_ref.at[e], sems.at[e])

    def each(do):
        def step(e, _):
            pl.when(used_ref[e] == 0)(lambda: do(e))
            return 0

        lax.fori_loop(0, out_ref.shape[0], step, 0)

    each(lambda e: copy(e).start())
    each(lambda e: copy(e).wait())


def clear_rest(used, tiles):
    wide, tile, _ = tiles.shape
    return pl.pallas_call(
        clear_kernel,
        in_specs=[SMEM, ANY],
        out_specs=ANY,
        out_shape=pltpu.HBM(tiles.shape, jnp.float32),
        scratch_shapes=[
            pltpu.VMEM((tile, tile), jnp.float32),
            pltpu.SemaphoreType.DMA((wide,)),
        ],
        input_output_aliases={1: 0},
        cost_estimate=pl.CostEstimate(flops=0, bytes_accessed=8 * MIB, transcendentals=0),
        compiler_params=params(LIMIT),
        name="clear",
    )(used, tiles)


def scale_kernel(used_ref, most_ref, _, out_ref, held, come, go):
    get = lambda e: pltpu.make_async_copy(out_ref.at[e], held.at[e], come.at[e])
    put = lambda e: pltpu.make_async_copy(held.at[e], out_ref.at[e], go.at[e])
    factor = 1.0 / (most_ref[0, 0] + 1e-06)

    def one(e):
        get(e).wait()
        held[e] = held[e] * factor
        put(e).start()

    each_used(used_ref, lambda e: get(e).start())
    each_used(used_ref, one)
    each_used(used_ref, lambda e: put(e).wait())


def scale(used, bound, tiles):
    return pl.pallas_call(
        scale_kernel,
        in_specs=[SMEM, SMEM, ANY],
        out_specs=ANY,
        out_shape=pltpu.HBM(tiles.shape, jnp.float32),
        scratch_shapes=[
            pltpu.VMEM(tiles.shape, jnp.float32),
            pltpu.SemaphoreType.DMA((tiles.shape[0],)),
            pltpu.SemaphoreType.DMA((tiles.shape[0],)),
        ],
        input_output_aliases={2: 0},
        compiler_params=params(LIMIT),
        name="scale",
    )(used, bound, tiles)


def wanted_ends(cols, owners, rows):
    cols = cols[..., None]
    hit = (cols >= 0) & (cols // rows == owners)
    low = jnp.min(jnp.where(hit, cols % rows, rows - 1), axis=(1, 2))
    high = jnp.max(jnp.where(hit, cols % rows, 0), axis=(1, 2))
    return low, high


def per_device(blocks, prolong, counts, columns, aggregates):
    rows, slots = columns.shape
    tile = blocks.shape[-1]
    ny, nz = lax.axis_size("col_0"), lax.axis_size("col_1")
    my_y, my_z = lax.axis_index("col_0"), lax.axis_index("col_1")
    peers = ny * nz
    wide = AGD * peers
    flat = rows * slots
    around = [[(i, (i + d) % nz) for i in range(nz)] for d in (1, -1)]
    hop = lambda x, way: lax.ppermute(x, "col_1", around[way])
    swap = lambda x, axis="col_0": lax.all_to_all(x, axis, split_axis=0, concat_axis=0, tiled=True)
    live = jnp.arange(slots, dtype=jnp.int32)[None, :] < counts[:, None]
    tags = jnp.broadcast_to(aggregates.astype(jnp.float32)[:, None, None], (rows, 8, tile))
    tagged = jnp.concatenate([prolong, tags], axis=1)
    up, down = hop(tagged, 0), hop(tagged, 1)
    note = jnp.where(live, columns, -1)
    theirs = swap(jnp.broadcast_to(note, (ny, *note.shape)))
    inner, done = inner_products(blocks, prolong)
    inner = inner.reshape(flat, 2 * tile, tile)
    apart = jnp.arange(nz, dtype=jnp.int32)
    owners = my_y * nz + (my_z + apart) % nz
    low, high = wanted_ends(theirs, owners, rows)
    picks = jnp.stack([low, high], axis=-1).reshape(ny, nz * CAP)
    held = {0: tagged}
    for r in range(1, nz // 2):
        held[nz - r], held[r] = up, down
        far = r == nz // 2 - 1
        up, down = (up[: rows // 2], down[rows // 2 :]) if far else (up, down)
        up, down = hop(up, 0), hop(down, 1)
    orders, parts = [[0]], []
    for r in range(1, nz // 2):
        orders[-1] += [nz - r, r]
        if r in CUTS:
            orders.append([])
    orders[-1].append(nz // 2)
    at = my_y[None]
    onward = lambda x, d: lax.ppermute(x, "col_0", [(i, (i + d) % ny) for i in range(ny)])
    for n, steps in enumerate(orders):
        last = nz // 2 in steps
        sets = [held[d] for d in steps if d in held] + ([up, down] if last else [])
        sent = pick(picks, at, sets, tuple(steps + steps[-1:] * last), n >= MERGED, (done,) * (n == EARLY))
        if n >= MERGED:
            parts += [sent[0]] + [onward(sent[d], d) for d in range(1, ny)]
        else:
            parts.append(swap(sent[0]).reshape(-1, *tagged.shape[1:]))
    cols = columns.reshape(1, flat)
    live = live.reshape(1, flat)
    owner, within = cols // rows, cols % rows
    same = (owner.T == owner) & live
    first = jnp.min(jnp.where(same, within, rows), axis=1)[None, :]
    second = (within > first).astype(jnp.int32)
    ahead = (owner % nz - my_z) % nz
    source, base = jnp.zeros_like(owner), 0
    for n, steps in enumerate(orders):
        peer = (my_y - owner // nz) % ny if n >= MERGED else owner // nz
        for s, step in enumerate(steps):
            there = base + (peer * len(steps) + s) * CAP + second
            source = jnp.where(ahead == step, there, source)
        base += len(steps) * ny * CAP
    row_agg = jnp.broadcast_to(aggregates[:, None], (rows, slots)).reshape(1, flat)
    target = row_agg * wide + owner * AGD
    number = jnp.arange(flat, dtype=jnp.int32)[None, :]
    place = jnp.sum(jnp.where((number < number.T) & live, 1, 0), axis=1)[:, None]
    moved = (place == number) & live.T
    front = lambda x, rest: jnp.sum(jnp.where(moved, x.T - rest, 0), axis=0)[None, :] + rest
    total = jnp.broadcast_to(jnp.sum(live.astype(jnp.int32)), (1, flat))
    where = jnp.concatenate(
        [front(number, 0), front(source, 0), front(target, AGD * wide), total], axis=0
    ).astype(jnp.int32)
    tiles, used, most = sum_terms(where, inner, parts, AGD * wide)
    everyone = lax.axis_size(ROW_COL)
    all_most = swap(jnp.broadcast_to(most, (everyone, tile)), ROW_COL)
    bound = jnp.max(all_most).reshape(1, 1)
    return scale(used, bound, clear_rest(used, tiles)).reshape(AGD, wide, tile, tile)


def solution(mesh):
    torus = Mesh(mesh.devices.reshape(4, 2, 4, 8), ("row_0", "row_1", "col_0", "col_1"))
    placed = (
        P(ROW_COL, None, None, None),
        P(ROW_COL, None, None),
        P(ROW_COL),
        P(ROW_COL, None),
        P(ROW_COL),
    )
    return jax.shard_map(
        per_device,
        mesh=torus,
        in_specs=placed,
        out_specs=P(ROW_COL, None, None, None),
        check_vma=False,
    )
```

```python
import functools

import jax
import jax.numpy as jnp
from jax import lax
from jax.experimental import pallas as pl
from jax.experimental.pallas import tpu as pltpu
from jax.sharding import Mesh
from jax.sharding import PartitionSpec as P

AGD = 2
CAP = 2
COL = ("col_0", "col_1")
ROW_COL = ("row_0", "row_1", "col_0", "col_1")
ANY = pl.BlockSpec(memory_space=pl.ANY)
SMEM = pl.BlockSpec(memory_space=pltpu.SMEM)
VMEM = pl.BlockSpec(memory_space=pltpu.VMEM)
HBM = pl.BlockSpec(memory_space=pltpu.HBM)
MIB = 1 << 20
UNROLL = 4
CHUNK = 8
CUTS = (1,2)
MERGED = 1
LIMIT = 60


def split(x, axis):
    hi = x.astype(jnp.bfloat16)
    lo = (x - hi.astype(jnp.float32)).astype(jnp.bfloat16)
    return jnp.concatenate([hi, lo], axis=axis)


def dot_split(left, right):
    n = right.shape[0]
    four = jnp.dot(left, right, preferred_element_type=jnp.float32)
    return four[:n, :n] + ((four[:n, n:] + four[n:, :n]) + four[n:, n:])


def params(mib):
    return pltpu.CompilerParams(vmem_limit_bytes=mib * MIB)


def inner_kernel(blocks_ref, prolong_ref, out_ref, done_ref):
    left = split(prolong_ref[0].T, 0)
    for k in range(blocks_ref.shape[1]):
        out_ref[0, k] = split(dot_split(left, split(blocks_ref[0, k], 1)), 0)
    done_ref[...] = jnp.zeros_like(done_ref)


def inner_products(blocks, prolong):
    rows, slots, tile, _ = blocks.shape
    return pl.pallas_call(
        inner_kernel,
        grid=(rows,),
        in_specs=[
            pl.BlockSpec((1, slots, tile, tile), lambda i: (i, 0, 0, 0)),
            pl.BlockSpec((1, tile, tile), lambda i: (i, 0, 0)),
        ],
        out_specs=[
            pl.BlockSpec((1, slots, 2 * tile, tile), lambda i: (i, 0, 0, 0)),
            pl.BlockSpec((8, tile), lambda i: (0, 0)),
        ],
        out_shape=[
            pltpu.HBM((rows, slots, 2 * tile, tile), jnp.bfloat16),
            jax.ShapeDtypeStruct((8, tile), jnp.float32),
        ],
        cost_estimate=pl.CostEstimate(
            flops=8 * rows * slots * tile**3, bytes_accessed=9 * MIB, transcendentals=0
        ),
        compiler_params=params(LIMIT),
        name="inner",
    )(blocks, prolong)


def pick_kernel(steps, apart, pick_ref, at_ref, *refs):
    peers = pick_ref.shape[0]
    count = peers if apart else 1
    sources, outs, (sets, sems) = refs[: len(steps)], refs[-2 - count : -2], refs[-2:]
    loads, place = [], {}
    at = 0
    for n, step in enumerate(steps):
        place[step] = place.get(step, at)
        count = sources[n].shape[0]
        loads.append(
            pltpu.make_async_copy(sources[n], sets.at[pl.ds(at, count)], sems.at[n])
        )
        at += count
    for load in loads:
        load.start()
    for n, load in enumerate(loads):
        load.wait()
        if steps[n] in steps[n + 1 :]:
            continue
        s = list(place).index(steps[n])
        for y in range(peers):
            for p in range(CAP):
                if apart:
                    out, peer = outs[y], (at_ref[0] + y) % peers
                else:
                    out, peer = outs[0].at[y], y
                out[CAP * s + p] = sets[place[steps[n]] + pick_ref[peer, CAP * steps[n] + p]]


def pick(picks, at, sets, steps, apart, after):
    peers = picks.shape[0]
    shape = (len(set(steps)) * CAP, *sets[0].shape[1:])
    shapes = [pltpu.HBM(shape, jnp.float32)] * peers
    return pl.pallas_call(
        functools.partial(pick_kernel, steps, apart),
        in_specs=[SMEM, SMEM] + [ANY] * (len(sets) + len(after)),
        out_specs=[VMEM] * peers if apart else [VMEM],
        out_shape=shapes if apart else [pltpu.HBM((peers, *shape), jnp.float32)],
        scratch_shapes=[
            pltpu.VMEM((sum(x.shape[0] for x in sets), *shape[1:]), jnp.float32),
            pltpu.SemaphoreType.DMA((len(sets),)),
        ],
        cost_estimate=pl.CostEstimate(flops=0, bytes_accessed=8 * MIB, transcendentals=0),
        compiler_params=params(LIMIT),
        name="pick",
    )(picks, at, *sets, *after)


def terms_kernel(first, final, parts_n, slot_ref, inner_ref, *refs):
    parts = refs[:parts_n]
    if final:
        old_ref, old_tiles = refs[parts_n : parts_n + 2]
        outs = refs[parts_n + 2 : parts_n + 5]
        most_ref = outs[2]
    else:
        outs = refs[parts_n : parts_n + 2]
    out_ref, used_ref = outs[:2]
    left, held, right, sums, most, ids, agg_ref, sem, sems, part_sems, left_sems = refs[-11:]
    wide = used_ref.shape[0] // 2 - 4
    spare, tile = out_ref.shape[0], out_ref.shape[-1]
    begin = slot_ref[3, 0] if final else 0
    end = begin + slot_ref[3, 1] if final else slot_ref[3, 0]

    def load(s):
        return pltpu.make_async_copy(inner_ref.at[slot_ref[0, s]], left.at[s], left_sems.at[s])

    def save(n):
        at = pl.ds(CHUNK * n, CHUNK)
        return pltpu.make_async_copy(sums.at[at], out_ref.at[at], sems.at[n])

    def back(n):
        at = pl.ds(CHUNK * n, CHUNK)
        return pltpu.make_async_copy(old_tiles.at[at], sums.at[at], sems.at[n])

    def loads(do):
        def step(s, _):
            do(load(s))
            return 0

        lax.fori_loop(begin, end, step, 0)

    copies = []
    at = 0
    for n, part in enumerate(parts):
        count = part.shape[0]
        copies.append(pltpu.make_async_copy(part, held.at[pl.ds(at, count)], part_sems.at[n]))
        copies[-1].start()
        at += count
    loads(lambda copy: copy.start())

    def fresh(e, _):
        for n in range(8):
            used_ref[8 * e + n] = old_ref[8 * e + n] if final else 0
        return 0

    lax.fori_loop(0, used_ref.shape[0] // 8, fresh, 0)
    if final:
        each_chunk(used_ref, lambda n: back(n).start())
    for copy in copies:
        copy.wait()
    for n in range(at):
        ids[n : n + 1] = held[n, tile : tile + 1].astype(jnp.int32)
    look_up = pltpu.make_async_copy(ids, agg_ref, sem)
    look_up.start()
    for n in range(at):
        right[n] = split(held[n, :tile], 1)
    loads(lambda copy: copy.wait())
    look_up.wait()
    if final:
        each_chunk(used_ref, lambda n: back(n).wait())

    def some(n, _):
        terms, places = [], []
        for m in range(UNROLL):
            s = begin + UNROLL * n + m
            inside = s < end
            s = jnp.where(inside, s, begin)
            source = jnp.clip(slot_ref[1, s] - first, 0, at - 1)
            places.append(jnp.where(inside, slot_ref[2, s] + agg_ref[source, 0], wide))
            terms.append(dot_split(left[s], right[source]))
        for e, term in zip(places, terms):

            @pl.when((e < wide) & (used_ref[jnp.minimum(e, wide - 1)] == 0))
            def _():
                count = used_ref[2 * wide]
                used_ref[wide + count] = e
                used_ref[2 * wide] = count + 1
                used_ref[e] = count + 1
                sums[count] = jnp.zeros((tile, tile), jnp.float32)

            n = jnp.where(e < wide, used_ref[jnp.minimum(e, wide - 1)] - 1, spare)
            sums[n] = sums[n] + term
        return 0

    sums[spare] = jnp.zeros((tile, tile), jnp.float32)
    lax.fori_loop(0, (end - begin + UNROLL - 1) // UNROLL, some, 0)
    each_chunk(used_ref, lambda n: save(n).start())
    if final:
        most[...] = jnp.zeros_like(most)
        half = wide // AGD

        def look(n, e):
            most[e // half] = most[e // half] + jnp.abs(sums[n])

        each_used(used_ref, look)
        row_sums = jnp.sum(most[...], axis=2)
        most_ref[...] = jnp.full(most_ref.shape, jnp.max(row_sums), jnp.float32)
    each_chunk(used_ref, lambda n: save(n).wait())


def each_used(used_ref, do):
    wide = used_ref.shape[0] // 2 - 4

    def step(n, _):
        do(n, used_ref[wide + n])
        return 0

    lax.fori_loop(0, used_ref[2 * wide], step, 0)


def each_chunk(used_ref, do):
    def step(n, _):
        do(n)
        return 0

    lax.fori_loop(0, (used_ref[used_ref.shape[0] - 8] + CHUNK - 1) // CHUNK, step, 0)


def sum_terms(slots, inner, parts, first, wide, everyone, before=()):
    flat, _, tile = inner.shape
    final = len(before) > 0
    count = sum(p.shape[0] for p in parts)
    return pl.pallas_call(
        functools.partial(terms_kernel, first, final, len(parts)),
        in_specs=[SMEM, ANY] + [ANY] * len(parts) + [SMEM, ANY] * final,
        out_specs=[ANY, SMEM] + [VMEM] * final,
        out_shape=[
            pltpu.HBM(inner.shape[:1] + (tile, tile), jnp.float32),
            jax.ShapeDtypeStruct((2 * wide + 8,), jnp.int32),
        ]
        + [jax.ShapeDtypeStruct((everyone, 1, tile), jnp.float32)] * final,
        scratch_shapes=[
            pltpu.VMEM(inner.shape, jnp.bfloat16),
            pltpu.VMEM((count, *parts[0].shape[1:]), jnp.float32),
            pltpu.VMEM((count, tile, 2 * tile), jnp.bfloat16),
            pltpu.VMEM((flat + 1, tile, tile), jnp.float32),
            pltpu.VMEM((AGD, tile, tile), jnp.float32),
            pltpu.VMEM((count, tile), jnp.int32),
            pltpu.SMEM((count, tile), jnp.int32),
            pltpu.SemaphoreType.DMA,
            pltpu.SemaphoreType.DMA((flat // CHUNK,)),
            pltpu.SemaphoreType.DMA((len(parts),)),
            pltpu.SemaphoreType.DMA((flat,)),
        ],
        cost_estimate=pl.CostEstimate(
            flops=8 * flat * tile**3, bytes_accessed=16 * MIB, transcendentals=0
        ),
        compiler_params=params(LIMIT),
        name="terms",
    )(slots, inner, *parts, *before)


def clear_kernel(used_ref, out_ref, zero, sems):
    zero[...] = jnp.zeros_like(zero)
    copy = lambda e: pltpu.make_async_copy(zero, out_ref.at[e], sems.at[e])

    def each(do):
        def step(e, _):
            pl.when(used_ref[e] == 0)(lambda: do(e))
            return 0

        lax.fori_loop(0, out_ref.shape[0], step, 0)

    each(lambda e: copy(e).start())
    each(lambda e: copy(e).wait())


def clear_rest(used, wide, tile):
    return pl.pallas_call(
        clear_kernel,
        in_specs=[SMEM],
        out_specs=ANY,
        out_shape=pltpu.HBM((wide, tile, tile), jnp.float32),
        scratch_shapes=[
            pltpu.VMEM((tile, tile), jnp.float32),
            pltpu.SemaphoreType.DMA((wide,)),
        ],
        cost_estimate=pl.CostEstimate(flops=0, bytes_accessed=8 * MIB, transcendentals=0),
        compiler_params=params(LIMIT),
        name="clear",
    )(used)


def scale_kernel(used_ref, most_ref, tiles_ref, _, out_ref, held, come, go):
    def get(n):
        at = pl.ds(CHUNK * n, CHUNK)
        return pltpu.make_async_copy(tiles_ref.at[at], held.at[at], come.at[n])

    put = lambda n, e: pltpu.make_async_copy(held.at[n], out_ref.at[e], go.at[n])
    each_chunk(used_ref, lambda n: get(n).start())
    factor = 1.0 / (jnp.max(most_ref[...]) + 1e-06)

    def one(n, e):
        pl.when(n % CHUNK == 0)(lambda: get(n // CHUNK).wait())
        held[n] = held[n] * factor
        put(n, e).start()

    each_used(used_ref, one)
    each_used(used_ref, lambda n, e: put(n, e).wait())


def scale(used, bound, tiles, cleared):
    return pl.pallas_call(
        scale_kernel,
        in_specs=[SMEM, VMEM, ANY, ANY],
        out_specs=ANY,
        out_shape=pltpu.HBM(cleared.shape, jnp.float32),
        scratch_shapes=[
            pltpu.VMEM(tiles.shape, jnp.float32),
            pltpu.SemaphoreType.DMA((tiles.shape[0] // CHUNK,)),
            pltpu.SemaphoreType.DMA((tiles.shape[0],)),
        ],
        input_output_aliases={3: 0},
        compiler_params=params(LIMIT),
        name="scale",
    )(used, bound, tiles, cleared)


def wanted_ends(cols, owners, rows):
    cols = cols[..., None]
    hit = (cols >= 0) & (cols // rows == owners)
    low = jnp.min(jnp.where(hit, cols % rows, rows - 1), axis=(1, 2))
    high = jnp.max(jnp.where(hit, cols % rows, 0), axis=(1, 2))
    return low, high


def per_device(blocks, prolong, counts, columns, aggregates):
    rows, slots = columns.shape
    tile = blocks.shape[-1]
    ny, nz = lax.axis_size("col_0"), lax.axis_size("col_1")
    my_y, my_z = lax.axis_index("col_0"), lax.axis_index("col_1")
    peers = ny * nz
    wide = AGD * peers
    flat = rows * slots
    around = [[(i, (i + d) % nz) for i in range(nz)] for d in (1, -1)]
    hop = lambda x, way: lax.ppermute(x, "col_1", around[way])
    swap = lambda x, axis="col_0": lax.all_to_all(x, axis, split_axis=0, concat_axis=0, tiled=True)
    live = jnp.arange(slots, dtype=jnp.int32)[None, :] < counts[:, None]
    tags = jnp.broadcast_to(aggregates.astype(jnp.float32)[:, None, None], (rows, 8, tile))
    tagged = jnp.concatenate([prolong, tags], axis=1)
    up, down = hop(tagged, 0), hop(tagged, 1)
    note = jnp.where(live, columns, -1)
    theirs = swap(jnp.broadcast_to(note, (ny, *note.shape)))
    inner, done = inner_products(blocks, prolong)
    inner = inner.reshape(flat, 2 * tile, tile)
    apart = jnp.arange(nz, dtype=jnp.int32)
    owners = my_y * nz + (my_z + apart) % nz
    low, high = wanted_ends(theirs, owners, rows)
    picks = jnp.stack([low, high], axis=-1).reshape(ny, nz * CAP)
    held = {0: tagged}
    for r in range(1, nz // 2):
        held[nz - r], held[r] = up, down
        far = r == nz // 2 - 1
        up, down = (up[: rows // 2], down[rows // 2 :]) if far else (up, down)
        up, down = hop(up, 0), hop(down, 1)
    orders, parts = [[0]], []
    for r in range(1, nz // 2):
        orders[-1] += [nz - r, r]
        if r in CUTS:
            orders.append([])
    orders[-1].append(nz // 2)
    at = my_y[None]
    onward = lambda x, d: lax.ppermute(x, "col_0", [(i, (i + d) % ny) for i in range(ny)])
    for n, steps in enumerate(orders):
        last = nz // 2 in steps
        sets = [held[d] for d in steps if d in held] + ([up, down] if last else [])
        after = (done,) if n == 0 else (parts[-1],) * last
        sent = pick(picks, at, sets, tuple(steps + steps[-1:] * last), n >= MERGED, after)
        if n >= MERGED:
            parts += [sent[0]] + [onward(sent[d], d) for d in range(1, ny)]
        else:
            parts.append(swap(sent[0]).reshape(-1, *tagged.shape[1:]))
    cols = columns.reshape(1, flat)
    live = live.reshape(1, flat)
    owner, within = cols // rows, cols % rows
    same = (owner.T == owner) & live
    first = jnp.min(jnp.where(same, within, rows), axis=1)[None, :]
    second = (within > first).astype(jnp.int32)
    ahead = (owner % nz - my_z) % nz
    source, base = jnp.zeros_like(owner), 0
    for n, steps in enumerate(orders):
        peer = (my_y - owner // nz) % ny if n >= MERGED else owner // nz
        for s, step in enumerate(steps):
            there = base + (peer * len(steps) + s) * CAP + second
            source = jnp.where(ahead == step, there, source)
        base += len(steps) * ny * CAP
    row_agg = jnp.broadcast_to(aggregates[:, None], (rows, slots)).reshape(1, flat)
    target = row_agg * wide + owner * AGD
    number = jnp.arange(flat, dtype=jnp.int32)[None, :]
    late_from = flat - len(orders[-1]) * ny * CAP
    early = live & (source < late_from)
    late = live & (source >= late_from)
    count = lambda x: jnp.sum(jnp.where((number < number.T) & x, 1, 0), axis=1)[:, None]
    early_total, late_total = (jnp.sum(x.astype(jnp.int32)) for x in (early, late))
    place = jnp.where(early.T, count(early), early_total + count(late))
    moved = (place == number) & live.T
    front = lambda x: jnp.sum(jnp.where(moved, x.T, 0), axis=0)[None, :]
    totals = jnp.where(number == 0, early_total, late_total)
    where = jnp.concatenate([front(number), front(source), front(target), totals], axis=0)
    where = where.astype(jnp.int32)
    everyone = lax.axis_size(ROW_COL)
    add = functools.partial(sum_terms, where, inner, wide=AGD * wide, everyone=everyone)
    at = len(parts) - ny
    tiles, used = add(parts[:at], 0)
    tiles, used, most = add(parts[at:], late_from, before=(used, tiles))
    all_most = swap(most, ROW_COL)
    cleared = clear_rest(used, AGD * wide, tile)
    return scale(used, all_most, tiles, cleared).reshape(AGD, wide, tile, tile)


def solution(mesh):
    torus = Mesh(mesh.devices.reshape(4, 2, 4, 8), ("row_0", "row_1", "col_0", "col_1"))
    placed = (
        P(ROW_COL, None, None, None),
        P(ROW_COL, None, None),
        P(ROW_COL),
        P(ROW_COL, None),
        P(ROW_COL),
    )
    return jax.shard_map(
        per_device,
        mesh=torus,
        in_specs=placed,
        out_specs=P(ROW_COL, None, None, None),
        check_vma=False,
    )
```

```python
import functools

import jax
import jax.numpy as jnp
from jax import lax
from jax.experimental import pallas as pl
from jax.experimental.pallas import tpu as pltpu
from jax.sharding import Mesh
from jax.sharding import PartitionSpec as P

AGD = 2
CAP = 2
COL = ("col_0", "col_1")
ROW_COL = ("row_0", "row_1", "col_0", "col_1")
ANY = pl.BlockSpec(memory_space=pl.ANY)
SMEM = pl.BlockSpec(memory_space=pltpu.SMEM)
VMEM = pl.BlockSpec(memory_space=pltpu.VMEM)
HBM = pl.BlockSpec(memory_space=pltpu.HBM)
MIB = 1 << 20
UNROLL = 8
CHUNK = 8
CUTS = (1,2)
MERGED = 1
LIMIT = 60


def split(x, axis):
    hi = x.astype(jnp.bfloat16)
    lo = (x - hi.astype(jnp.float32)).astype(jnp.bfloat16)
    return jnp.concatenate([hi, lo], axis=axis)


def dot_split(left, right):
    n = left.shape[0]
    left = jnp.concatenate([left, left[:, :n]], axis=1)
    right = jnp.concatenate([right[:n], right], axis=0)
    return jnp.dot(left, right, preferred_element_type=jnp.float32)


def params(mib):
    return pltpu.CompilerParams(vmem_limit_bytes=mib * MIB)


def inner_kernel(blocks_ref, prolong_ref, out_ref, done_ref):
    left = split(prolong_ref[0].T, 1)
    for k in range(blocks_ref.shape[1]):
        out_ref[0, k] = split(dot_split(left, split(blocks_ref[0, k], 0)), 1)
    done_ref[...] = jnp.zeros_like(done_ref)


def inner_products(blocks, prolong):
    rows, slots, tile, _ = blocks.shape
    return pl.pallas_call(
        inner_kernel,
        grid=(rows,),
        in_specs=[
            pl.BlockSpec((1, slots, tile, tile), lambda i: (i, 0, 0, 0)),
            pl.BlockSpec((1, tile, tile), lambda i: (i, 0, 0)),
        ],
        out_specs=[
            pl.BlockSpec((1, slots, tile, 2 * tile), lambda i: (i, 0, 0, 0)),
            pl.BlockSpec((8, tile), lambda i: (0, 0)),
        ],
        out_shape=[
            pltpu.HBM((rows, slots, tile, 2 * tile), jnp.bfloat16),
            jax.ShapeDtypeStruct((8, tile), jnp.float32),
        ],
        cost_estimate=pl.CostEstimate(
            flops=8 * rows * slots * tile**3, bytes_accessed=9 * MIB, transcendentals=0
        ),
        compiler_params=params(LIMIT),
        name="inner",
    )(blocks, prolong)


def pick_kernel(steps, apart, pick_ref, at_ref, *refs):
    peers = pick_ref.shape[0]
    count = peers if apart else 1
    sources, outs, (sets, sems) = refs[: len(steps)], refs[-2 - count : -2], refs[-2:]
    loads, place = [], {}
    at = 0
    for n, step in enumerate(steps):
        place[step] = place.get(step, at)
        count = sources[n].shape[0]
        loads.append(
            pltpu.make_async_copy(sources[n], sets.at[pl.ds(at, count)], sems.at[n])
        )
        at += count
    for load in loads:
        load.start()
    for n, load in enumerate(loads):
        load.wait()
        if steps[n] in steps[n + 1 :]:
            continue
        s = list(place).index(steps[n])
        for y in range(peers):
            for p in range(CAP):
                if apart:
                    out, peer = outs[y], (at_ref[0] + y) % peers
                else:
                    out, peer = outs[0].at[y], y
                out[CAP * s + p] = sets[place[steps[n]] + pick_ref[peer, CAP * steps[n] + p]]


def pick(picks, at, sets, steps, apart, after):
    peers = picks.shape[0]
    shape = (len(set(steps)) * CAP, *sets[0].shape[1:])
    shapes = [pltpu.HBM(shape, jnp.float32)] * peers
    return pl.pallas_call(
        functools.partial(pick_kernel, steps, apart),
        in_specs=[SMEM, SMEM] + [ANY] * (len(sets) + len(after)),
        out_specs=[VMEM] * peers if apart else [VMEM],
        out_shape=shapes if apart else [pltpu.HBM((peers, *shape), jnp.float32)],
        scratch_shapes=[
            pltpu.VMEM((sum(x.shape[0] for x in sets), *shape[1:]), jnp.float32),
            pltpu.SemaphoreType.DMA((len(sets),)),
        ],
        cost_estimate=pl.CostEstimate(flops=0, bytes_accessed=8 * MIB, transcendentals=0),
        compiler_params=params(LIMIT),
        name="pick",
    )(picks, at, *sets, *after)


def terms_kernel(first, final, parts_n, slot_ref, inner_ref, *refs):
    parts = refs[:parts_n]
    if final:
        old_ref, old_tiles = refs[parts_n : parts_n + 2]
        outs = refs[parts_n + 2 : parts_n + 5]
        most_ref = outs[2]
    else:
        outs = refs[parts_n : parts_n + 2]
    out_ref, used_ref = outs[:2]
    left, held, right, sums, most, ids, agg_ref, sem, sems, part_sems, left_sems = refs[-11:]
    wide = used_ref.shape[0] // 2 - 4
    spare, tile = out_ref.shape[0], out_ref.shape[-1]
    begin = slot_ref[3, 0] if final else 0
    end = begin + slot_ref[3, 1] if final else slot_ref[3, 0]

    def load(s):
        return pltpu.make_async_copy(inner_ref.at[slot_ref[0, s]], left.at[s], left_sems.at[s])

    def save(n):
        at = pl.ds(CHUNK * n, CHUNK)
        return pltpu.make_async_copy(sums.at[at], out_ref.at[at], sems.at[n])

    def back(n):
        at = pl.ds(CHUNK * n, CHUNK)
        return pltpu.make_async_copy(old_tiles.at[at], sums.at[at], sems.at[n])

    def loads(do):
        def step(s, _):
            do(load(s))
            return 0

        lax.fori_loop(begin, end, step, 0)

    copies = []
    at = 0
    for n, part in enumerate(parts):
        count = part.shape[0]
        copies.append(pltpu.make_async_copy(part, held.at[pl.ds(at, count)], part_sems.at[n]))
        copies[-1].start()
        at += count
    loads(lambda copy: copy.start())

    def fresh(e, _):
        for n in range(8):
            used_ref[8 * e + n] = old_ref[8 * e + n] if final else 0
        return 0

    lax.fori_loop(0, used_ref.shape[0] // 8, fresh, 0)
    if final:
        each_chunk(used_ref, lambda n: back(n).start())
    for copy in copies:
        copy.wait()
    for n in range(at):
        ids[n : n + 1] = held[n, tile : tile + 1].astype(jnp.int32)
    look_up = pltpu.make_async_copy(ids, agg_ref, sem)
    look_up.start()
    for n in range(at):
        right[n] = split(held[n, :tile], 0)
    loads(lambda copy: copy.wait())
    look_up.wait()
    if final:
        each_chunk(used_ref, lambda n: back(n).wait())

    def some(n, _):
        terms, places = [], []
        for m in range(UNROLL):
            s = begin + UNROLL * n + m
            inside = s < end
            s = jnp.where(inside, s, begin)
            source = jnp.clip(slot_ref[1, s] - first, 0, at - 1)
            places.append(jnp.where(inside, slot_ref[2, s] + agg_ref[source, 0], wide))
            terms.append(dot_split(left[s], right[source]))
        for e, term in zip(places, terms):

            @pl.when((e < wide) & (used_ref[jnp.minimum(e, wide - 1)] == 0))
            def _():
                count = used_ref[2 * wide]
                used_ref[wide + count] = e
                used_ref[2 * wide] = count + 1
                used_ref[e] = count + 1
                sums[count] = jnp.zeros((tile, tile), jnp.float32)

            n = jnp.where(e < wide, used_ref[jnp.minimum(e, wide - 1)] - 1, spare)
            sums[n] = sums[n] + term
        return 0

    sums[spare] = jnp.zeros((tile, tile), jnp.float32)
    lax.fori_loop(0, (end - begin + UNROLL - 1) // UNROLL, some, 0)
    each_chunk(used_ref, lambda n: save(n).start())
    if final:
        most[...] = jnp.zeros_like(most)
        half = wide // AGD

        def look(n, e):
            most[e // half] = most[e // half] + jnp.abs(sums[n])

        each_used(used_ref, look)
        row_sums = jnp.sum(most[...], axis=2)
        most_ref[...] = jnp.full(most_ref.shape, jnp.max(row_sums), jnp.float32)
    each_chunk(used_ref, lambda n: save(n).wait())


def each_used(used_ref, do):
    wide = used_ref.shape[0] // 2 - 4

    def step(n, _):
        do(n, used_ref[wide + n])
        return 0

    lax.fori_loop(0, used_ref[2 * wide], step, 0)


def each_chunk(used_ref, do):
    def step(n, _):
        do(n)
        return 0

    lax.fori_loop(0, (used_ref[used_ref.shape[0] - 8] + CHUNK - 1) // CHUNK, step, 0)


def sum_terms(slots, inner, parts, first, wide, everyone, before=()):
    flat, tile, _ = inner.shape
    final = len(before) > 0
    count = sum(p.shape[0] for p in parts)
    return pl.pallas_call(
        functools.partial(terms_kernel, first, final, len(parts)),
        in_specs=[SMEM, ANY] + [ANY] * len(parts) + [SMEM, ANY] * final,
        out_specs=[ANY, SMEM] + [VMEM] * final,
        out_shape=[
            pltpu.HBM(inner.shape[:1] + (tile, tile), jnp.float32),
            jax.ShapeDtypeStruct((2 * wide + 8,), jnp.int32),
        ]
        + [jax.ShapeDtypeStruct((everyone, 1, tile), jnp.float32)] * final,
        scratch_shapes=[
            pltpu.VMEM(inner.shape, jnp.bfloat16),
            pltpu.VMEM((count, *parts[0].shape[1:]), jnp.float32),
            pltpu.VMEM((count, 2 * tile, tile), jnp.bfloat16),
            pltpu.VMEM((flat + 1, tile, tile), jnp.float32),
            pltpu.VMEM((AGD, tile, tile), jnp.float32),
            pltpu.VMEM((count, tile), jnp.int32),
            pltpu.SMEM((count, tile), jnp.int32),
            pltpu.SemaphoreType.DMA,
            pltpu.SemaphoreType.DMA((flat // CHUNK,)),
            pltpu.SemaphoreType.DMA((len(parts),)),
            pltpu.SemaphoreType.DMA((flat,)),
        ],
        cost_estimate=pl.CostEstimate(
            flops=8 * flat * tile**3, bytes_accessed=16 * MIB, transcendentals=0
        ),
        compiler_params=params(LIMIT),
        name="terms",
    )(slots, inner, *parts, *before)


def clear_kernel(used_ref, out_ref, zero, sems):
    zero[...] = jnp.zeros_like(zero)
    copy = lambda e: pltpu.make_async_copy(zero, out_ref.at[e], sems.at[e])

    def each(do):
        def step(e, _):
            pl.when(used_ref[e] == 0)(lambda: do(e))
            return 0

        lax.fori_loop(0, out_ref.shape[0], step, 0)

    each(lambda e: copy(e).start())
    each(lambda e: copy(e).wait())


def clear_rest(used, wide, tile):
    return pl.pallas_call(
        clear_kernel,
        in_specs=[SMEM],
        out_specs=ANY,
        out_shape=pltpu.HBM((wide, tile, tile), jnp.float32),
        scratch_shapes=[
            pltpu.VMEM((tile, tile), jnp.float32),
            pltpu.SemaphoreType.DMA((wide,)),
        ],
        cost_estimate=pl.CostEstimate(flops=0, bytes_accessed=8 * MIB, transcendentals=0),
        compiler_params=params(LIMIT),
        name="clear",
    )(used)


def scale_kernel(used_ref, most_ref, tiles_ref, _, out_ref, held, come, go):
    def get(n):
        at = pl.ds(CHUNK * n, CHUNK)
        return pltpu.make_async_copy(tiles_ref.at[at], held.at[at], come.at[n])

    put = lambda n, e: pltpu.make_async_copy(held.at[n], out_ref.at[e], go.at[n])
    each_chunk(used_ref, lambda n: get(n).start())
    factor = 1.0 / (jnp.max(most_ref[...]) + 1e-06)

    def one(n, e):
        pl.when(n % CHUNK == 0)(lambda: get(n // CHUNK).wait())
        held[n] = held[n] * factor
        put(n, e).start()

    each_used(used_ref, one)
    each_used(used_ref, lambda n, e: put(n, e).wait())


def scale(used, bound, tiles, cleared):
    return pl.pallas_call(
        scale_kernel,
        in_specs=[SMEM, VMEM, ANY, ANY],
        out_specs=ANY,
        out_shape=pltpu.HBM(cleared.shape, jnp.float32),
        scratch_shapes=[
            pltpu.VMEM(tiles.shape, jnp.float32),
            pltpu.SemaphoreType.DMA((tiles.shape[0] // CHUNK,)),
            pltpu.SemaphoreType.DMA((tiles.shape[0],)),
        ],
        input_output_aliases={3: 0},
        compiler_params=params(LIMIT),
        name="scale",
    )(used, bound, tiles, cleared)


def wanted_ends(cols, owners, rows):
    cols = cols[..., None]
    hit = (cols >= 0) & (cols // rows == owners)
    low = jnp.min(jnp.where(hit, cols % rows, rows - 1), axis=(1, 2))
    high = jnp.max(jnp.where(hit, cols % rows, 0), axis=(1, 2))
    return low, high


def per_device(blocks, prolong, counts, columns, aggregates):
    rows, slots = columns.shape
    tile = blocks.shape[-1]
    ny, nz = lax.axis_size("col_0"), lax.axis_size("col_1")
    my_y, my_z = lax.axis_index("col_0"), lax.axis_index("col_1")
    peers = ny * nz
    wide = AGD * peers
    flat = rows * slots
    around = [[(i, (i + d) % nz) for i in range(nz)] for d in (1, -1)]
    hop = lambda x, way: lax.ppermute(x, "col_1", around[way])
    swap = lambda x, axis="col_0": lax.all_to_all(x, axis, split_axis=0, concat_axis=0, tiled=True)
    live = jnp.arange(slots, dtype=jnp.int32)[None, :] < counts[:, None]
    tags = jnp.broadcast_to(aggregates.astype(jnp.float32)[:, None, None], (rows, 8, tile))
    tagged = jnp.concatenate([prolong, tags], axis=1)
    up, down = hop(tagged, 0), hop(tagged, 1)
    note = jnp.where(live, columns, -1)
    theirs = swap(jnp.broadcast_to(note, (ny, *note.shape)))
    inner, done = inner_products(blocks, prolong)
    inner = inner.reshape(flat, tile, 2 * tile)
    apart = jnp.arange(nz, dtype=jnp.int32)
    owners = my_y * nz + (my_z + apart) % nz
    low, high = wanted_ends(theirs, owners, rows)
    picks = jnp.stack([low, high], axis=-1).reshape(ny, nz * CAP)
    held = {0: tagged}
    for r in range(1, nz // 2):
        held[nz - r], held[r] = up, down
        far = r == nz // 2 - 1
        up, down = (up[: rows // 2], down[rows // 2 :]) if far else (up, down)
        up, down = hop(up, 0), hop(down, 1)
    orders, parts = [[0]], []
    for r in range(1, nz // 2):
        orders[-1] += [nz - r, r]
        if r in CUTS:
            orders.append([])
    orders[-1].append(nz // 2)
    at = my_y[None]
    onward = lambda x, d: lax.ppermute(x, "col_0", [(i, (i + d) % ny) for i in range(ny)])
    for n, steps in enumerate(orders):
        last = nz // 2 in steps
        sets = [held[d] for d in steps if d in held] + ([up, down] if last else [])
        after = (done,) if n == 0 else (parts[-1],) * last
        sent = pick(picks, at, sets, tuple(steps + steps[-1:] * last), n >= MERGED, after)
        if n >= MERGED:
            parts += [sent[0]] + [onward(sent[d], d) for d in range(1, ny)]
        else:
            parts.append(swap(sent[0]).reshape(-1, *tagged.shape[1:]))
    cols = columns.reshape(1, flat)
    live = live.reshape(1, flat)
    owner, within = cols // rows, cols % rows
    same = (owner.T == owner) & live
    first = jnp.min(jnp.where(same, within, rows), axis=1)[None, :]
    second = (within > first).astype(jnp.int32)
    ahead = (owner % nz - my_z) % nz
    source, base = jnp.zeros_like(owner), 0
    for n, steps in enumerate(orders):
        peer = (my_y - owner // nz) % ny if n >= MERGED else owner // nz
        for s, step in enumerate(steps):
            there = base + (peer * len(steps) + s) * CAP + second
            source = jnp.where(ahead == step, there, source)
        base += len(steps) * ny * CAP
    row_agg = jnp.broadcast_to(aggregates[:, None], (rows, slots)).reshape(1, flat)
    target = row_agg * wide + owner * AGD
    number = jnp.arange(flat, dtype=jnp.int32)[None, :]
    late_from = flat - len(orders[-1]) * ny * CAP
    early = live & (source < late_from)
    late = live & (source >= late_from)
    count = lambda x: jnp.sum(jnp.where((number < number.T) & x, 1, 0), axis=1)[:, None]
    early_total, late_total = (jnp.sum(x.astype(jnp.int32)) for x in (early, late))
    place = jnp.where(early.T, count(early), early_total + count(late))
    moved = (place == number) & live.T
    front = lambda x: jnp.sum(jnp.where(moved, x.T, 0), axis=0)[None, :]
    totals = jnp.where(number == 0, early_total, late_total)
    where = jnp.concatenate([front(number), front(source), front(target), totals], axis=0)
    where = where.astype(jnp.int32)
    everyone = lax.axis_size(ROW_COL)
    add = functools.partial(sum_terms, where, inner, wide=AGD * wide, everyone=everyone)
    at = len(parts) - ny
    tiles, used = add(parts[:at], 0)
    tiles, used, most = add(parts[at:], late_from, before=(used, tiles))
    all_most = swap(most, ROW_COL)
    cleared = clear_rest(used, AGD * wide, tile)
    return scale(used, all_most, tiles, cleared).reshape(AGD, wide, tile, tile)


def solution(mesh):
    torus = Mesh(mesh.devices.reshape(4, 2, 4, 8), ("row_0", "row_1", "col_0", "col_1"))
    placed = (
        P(ROW_COL, None, None, None),
        P(ROW_COL, None, None),
        P(ROW_COL),
        P(ROW_COL, None),
        P(ROW_COL),
    )
    return jax.shard_map(
        per_device,
        mesh=torus,
        in_specs=placed,
        out_specs=P(ROW_COL, None, None, None),
        check_vma=False,
    )
```
